512 devices in a mesh: gy: 32 (over z_lo, y, core), gx: 16 (over x, z_hi).
Axes of the slice: x: 4, y: 4, z: 16 (z_hi: 4, z_lo: 4; z = z_hi * 4 + z_lo), core: 2. Of those that a mesh axis runs over, the one named last changes fastest.
Arguments:
- field: float32 [16, 2048, 2048], P(None, 'gy', 'gx'), may hold values from 0 to 1, as said below
- targets: float32 [3, 16], replicated, may hold values from 0.1 to 0.45
- weights: float32 [3, 16], replicated, may hold values from 0.3 to 3
Outputs:
- gradient: float32 [16, 2048, 2048], P(None, 'gy', 'gx')
- correlation: float32 [3, 16], replicated
The draws below stay inside these ranges and needn't reach their ends.
Inputs may be any that keep to these rules, and one draw needn't show every extreme that they name: `field`: every value lies strictly between 0 and 1.
All inputs are finite; a program needn't handle non-finite values.
Results may differ from the reference program's by a relative error of at most 0.00028.
Values sent between devices are 32-bit elements; how exact they have to be, the bound alone decides.
No kernel may reach another device: no remote copies, remote signals or barrier semaphores. Data moves between devices by JAX's collectives and lax.ppermute only.
A program may use at most 128 MiB of HBM per device.

```python
import math
import jax
import jax.numpy as jnp

OFFSETS = 16
PLANES = 16
NY = 2048
NX = 2048
VOXELS = 67108864


def box_variance(first, second):
    lower = min(first, second)
    upper = max(first, second)
    ramp = 0
    for count in range(1, lower):
        ramp = ramp + count * count
    return float(2 * ramp + lower * lower * (upper - lower + 1))


def box_sum(values, axis, width):
    total = values
    for offset in range(1, width):
        total = total + jnp.roll(values, offset, axis=axis)
    return total


def smoothed(noise, widths):
    values = noise
    for axis in range(3):
        first = widths[axis][0]
        second = widths[axis][1]
        values = box_sum(box_sum(values, axis, first), axis, second)
        values = values / jnp.float32(math.sqrt(box_variance(first, second)))
    return values


def draw_field(key, part):
    key = jax.random.fold_in(key, 7)
    rough_key = jax.random.fold_in(key, 11)
    smooth_key = jax.random.fold_in(key, 13)
    rows = jnp.arange(NY, dtype=jnp.float32) / jnp.float32(max(NY - 1, 1))
    rough = jax.random.normal(rough_key, (PLANES, NY, NX), jnp.float32)
    base = jax.random.normal(smooth_key, (PLANES, NY, NX), jnp.float32)
    widths = ((5, 9), (7, 11), (9, 13))
    amplitude = 0.7 * jnp.exp(math.log(3.0) * rows)
    mixed = 0.8 * smoothed(base, widths) + 0.6 * rough
    values = 0.5 + 0.49 * jnp.tanh(amplitude[None, :, None] * mixed)
    return values.astype(jnp.float32)


def setup_inputs(seed: int = 0) -> dict:
    arg_keys = jax.random.split(jax.random.key(seed), 4)
    field = draw_field(jax.random.fold_in(arg_keys[3], 71), 0)
    targets = jnp.clip(jax.random.uniform(arg_keys[1], (3, OFFSETS), jnp.float32, 0.1, 0.45), 0.1, 0.45)
    weights = jnp.clip(jnp.exp(jax.random.uniform(arg_keys[2], (3, OFFSETS), jnp.float32, math.log(0.3), math.log(3.0))), 0.3, 3.0)
    return {"field": field, "targets": targets, "weights": weights}


def plane_shift(field, by):
    planes = field.shape[0]
    zeros = jnp.zeros((abs(by),) + field.shape[1:], jnp.float32)
    if by > 0:
        return jnp.concatenate([field[by:], zeros], axis=0)
    if by < 0:
        return jnp.concatenate([zeros, field[:planes + by]], axis=0)
    return field


def reference(field, targets, weights):
    sums = []
    for axis in range(3):
        row = []
        for step in range(OFFSETS):
            if axis == 0:
                other = plane_shift(field, step)
            else:
                other = jnp.roll(field, -step, axis=axis)
            row.append(jnp.sum(field * other))
        sums.append(jnp.stack(row))
    correlation = jnp.stack(sums) / jnp.float32(VOXELS)
    coefficient = weights * (correlation - targets)
    gradient = jnp.zeros_like(field)
    for axis in range(3):
        for step in range(OFFSETS):
            if axis == 0:
                pair = plane_shift(field, step) + plane_shift(field, -step)
            else:
                pair = jnp.roll(field, -step, axis=axis) + jnp.roll(field, step, axis=axis)
            gradient = gradient + coefficient[axis, step] * pair
    return gradient, correlation
```

```python
import numpy as np
import jax
import jax.numpy as jnp
from jax import lax
from jax.sharding import Mesh, PartitionSpec as P

OFFSETS = 16
GY = ("zl", "y", "c")
GX = ("x", "zh")


def shift(block, axes, forward):
    count = lax.axis_size(axes)
    step = 1 if forward else count - 1
    return lax.ppermute(block, axes, [(i, (i + step) % count) for i in range(count)])


def plane_shift(field, by):
    planes = field.shape[0]
    zeros = jnp.zeros((abs(by),) + field.shape[1:], jnp.float32)
    if by > 0:
        return jnp.concatenate([field[by:], zeros], axis=0)
    if by < 0:
        return jnp.concatenate([zeros, field[: planes + by]], axis=0)
    return field


def group_sum(values, axes):
    count = lax.axis_size(axes)
    copies = jnp.broadcast_to(values[None], (count,) + values.shape)
    return lax.all_to_all(copies, axes, 0, 0).sum(0)


def on_device(field, targets, weights):
    planes, rows, cols = field.shape
    width = OFFSETS - 1
    voxels = planes * rows * cols * lax.axis_size(GY + GX)
    right = shift(field[:, :, :width], GX, False)
    below = shift(field[:, :width, :], GY, False)
    left = shift(field[:, :, cols - width :], GX, True)
    above = shift(field[:, rows - width :, :], GY, True)
    along_rows = jnp.concatenate([above, field, below], axis=1)
    along_cols = jnp.concatenate([left, field, right], axis=2)
    plane_terms = []
    row_terms = []
    col_terms = []
    for step in range(OFFSETS):
        plane_terms.append(jnp.sum(field * plane_shift(field, step)))
        row_terms.append(jnp.sum(field * along_rows[:, width + step : width + step + rows, :]))
        col_terms.append(jnp.sum(field * along_cols[:, :, width + step : width + step + cols]))
    partial_sums = jnp.stack([jnp.stack(plane_terms), jnp.stack(row_terms), jnp.stack(col_terms)])
    packed = jnp.pad(partial_sums, ((0, 5), (0, 112)))
    totals = group_sum(group_sum(packed, ("c", "y", "x")), ("zl", "zh"))[:3, :OFFSETS]
    correlation = totals / jnp.float32(voxels)
    coefficient = weights * (correlation - targets)
    gradient = jnp.zeros_like(field)
    for step in range(OFFSETS):
        gradient = gradient + coefficient[0, step] * (
            plane_shift(field, step) + plane_shift(field, -step)
        )
    for step in range(OFFSETS):
        forward_rows = along_rows[:, width + step : width + step + rows, :]
        backward_rows = along_rows[:, width - step : width - step + rows, :]
        forward_cols = along_cols[:, :, width + step : width + step + cols]
        backward_cols = along_cols[:, :, width - step : width - step + cols]
        gradient = gradient + coefficient[1, step] * (forward_rows + backward_rows)
        gradient = gradient + coefficient[2, step] * (forward_cols + backward_cols)
    return (gradient, correlation)


def solution(mesh):
    devices = np.asarray(mesh.devices).reshape(4, 4, 2, 4, 4)
    fine = Mesh(devices, GY + GX)
    return jax.shard_map(
        on_device,
        mesh=fine,
        in_specs=(P(None, GY, GX), P(), P()),
        out_specs=(P(None, GY, GX), P()),
        check_vma=False,
    )
```

```python
import jax
import jax.numpy as jnp
import numpy as np
from jax import lax
from jax.experimental import pallas as pl
from jax.experimental.pallas import tpu as pltpu
from jax.sharding import Mesh, PartitionSpec as P

OFFSETS = 16
GY = ("zl", "y", "c")
GX = ("x", "zh")
PLANE = ("c", "y", "x")
LINE = ("zl", "zh")
PLANES, ROWS, COLS = 16, 64, 128
GROUPS = 8
F32, BF16 = jnp.float32, jnp.bfloat16
HBM_SPEC = pl.BlockSpec(memory_space=pl.ANY)


def iota(shape, dim):
    return lax.broadcasted_iota(jnp.int32, shape, dim)


def halves(values):
    high = values.astype(BF16)
    return high, (values - high.astype(F32)).astype(BF16)


def contract(left, right, dims):
    return lax.dot_general(left, right, (dims, ((), ())), preferred_element_type=F32)


def quadrants(gram):
    half = gram.shape[0] // 2
    tall = gram[:half] + gram[half:]
    return tall[:, :half] + tall[:, half:] if half == 128 else tall + pltpu.roll(tall, half, 1)


def diagonal_sums(gram, keep, base):
    gram = jnp.where(keep, gram, 0.0)
    total = jnp.zeros((8, 128), F32)
    for block in range(gram.shape[0] // 8):
        by = (base - 8 * block) % 128
        values = gram[8 * block : 8 * block + 8]
        total = total + (pltpu.roll(values, by, 1) if by else values)
    row = iota((8, 128), 0)
    for bit in (1, 2, 4):
        total = jnp.where(row & bit != 0, pltpu.roll(total, 128 - bit, 1), total)
    return jnp.sum(total, axis=0, keepdims=True)


def edges_kernel(field, top, bottom, first, last):
    top[...] = field[:, :OFFSETS, :]
    bottom[...] = field[:, ROWS - OFFSETS :, :]
    block = iota((128, COLS), 1) // OFFSETS
    first_cols = jnp.zeros((128, COLS), F32)
    last_cols = jnp.zeros((128, COLS), F32)
    for group in range(GROUPS):
        values = field[2 * group : 2 * group + 2].reshape(128, COLS)
        moved = pltpu.roll(values, OFFSETS * group, 1) if group else values
        first_cols = jnp.where(block == group, moved, first_cols)
        last_cols = jnp.where(block == (group + 7) % 8, moved, last_cols)
    first[...] = first_cols
    last[...] = last_cols


def inner_kernel(field, out):
    gram = jnp.zeros((256, 256), F32)
    for part in range(ROWS // 8):
        values = field[:, 8 * part : 8 * part + 8, :].reshape(128, COLS)
        both = jnp.concatenate(halves(values), axis=0)
        gram = gram + contract(both, both, ((1,), (1,)))
    row, col = iota((128, 128), 0), iota((128, 128), 1)
    spread = diagonal_sums(quadrants(gram), (row % 8 == col % 8) & (col >= row), 0)
    gram = jnp.zeros((128, 128), F32)
    for plane in range(PLANES):
        both = jnp.concatenate(halves(field[plane]), axis=0)
        gram = gram + contract(both, both, ((1,), (1,)))
    apart = (col - row)[:ROWS]
    along_rows = diagonal_sums(quadrants(gram), (apart >= 0) & (apart < OFFSETS) & (col[:ROWS] < ROWS), 0)
    gram = jnp.zeros((256, 256), F32)
    for group in range(GROUPS):
        both = jnp.concatenate(halves(field[2 * group : 2 * group + 2].reshape(128, COLS)), axis=1)
        gram = gram + contract(both, both, ((0,), (0,)))
    apart = col - row
    along_cols = diagonal_sums(quadrants(gram), (apart >= 0) & (apart < OFFSETS), 0)
    lane, offset = iota((OFFSETS, 128), 1), iota((OFFSETS, 128), 0)
    column = jnp.sum(jnp.where(lane == 8 * offset, spread, 0.0), axis=1, keepdims=True)
    along_planes = jnp.sum(jnp.where(lane == offset, column, 0.0), axis=0, keepdims=True)
    axis = iota((8, 128), 0)
    sums = jnp.where(axis == 0, along_planes, jnp.where(axis == 1, along_rows, along_cols))
    out[...] = jnp.where((axis < 3) & (iota((8, 128), 1) < OFFSETS), sums, 0.0)


def border_kernel(inner, bottom, below, last, right, out):
    row, col = iota((128, 128), 0), iota((128, 128), 1)
    gram = jnp.zeros((128, 128), F32)
    for planes in (slice(0, 8), slice(8, 16)):
        mine_high, mine_low = halves(bottom[planes].reshape(128, COLS))
        next_high, next_low = halves(below[planes].reshape(128, COLS))
        product = contract(mine_high, jnp.concatenate([next_high, next_low], axis=0), ((1,), (1,)))
        gram = gram + product[:, :128] + product[:, 128:]
        gram = gram + contract(mine_low, next_high, ((1,), (1,)))
    along_rows = diagonal_sums(gram, (row // 16 == col // 16) & (col < row), OFFSETS)
    mine = jnp.concatenate(halves(last[...]), axis=1)
    other = jnp.concatenate(halves(right[...]), axis=1)
    gram = quadrants(contract(mine, other, ((0,), (0,))))
    apart = (col - row + 128) % 128
    keep = ((row // 16 + 1) % 8 == col // 16) & (apart < OFFSETS) & (apart > 0)
    along_cols = diagonal_sums(gram, keep, 0)
    axis = iota((8, 128), 0)
    sums = jnp.where(axis == 1, along_rows, jnp.where(axis == 2, along_cols, 0.0))
    sums = jnp.where(iota((8, 128), 1) < OFFSETS, sums, 0.0) + inner[...]
    out[...] = jnp.broadcast_to(sums[None], out.shape)


def gradient_kernel(
    voxels, field, above, below, left, right, totals, targets, weights, gradient, correlation, result, sems
):
    value = jnp.sum(totals[...], axis=0) / jnp.float32(voxels)
    correlation[...] = value[:3, :OFFSETS]
    coefficient = weights[...] * (value - targets[...])
    lane, offset = iota((OFFSETS, 128), 1), iota((OFFSETS, 128), 0)

    def column(axis):
        return jnp.sum(
            jnp.where(lane == offset, coefficient[axis : axis + 1], 0.0), axis=1, keepdims=True
        )

    def line(values, lanes):
        return jnp.sum(jnp.where(lane == lanes, values, 0.0), axis=0, keepdims=True)

    def toeplitz(values, size, base):
        return pltpu.roll(
            jnp.broadcast_to(values, (size, 128)), base, 1, stride=1, stride_axis=0
        )

    back = (128 - offset) % 128
    by_plane, by_row, by_col = column(0), column(1), column(2)
    row, col = iota((128, 128), 0), iota((128, 128), 1)
    ahead = toeplitz(line(by_plane, 8 * offset), 128, 0)
    behind = toeplitz(line(by_plane, (128 - 8 * offset) % 128), 128, 0)
    plane_high, plane_low = halves(
        jnp.where(col == row, 2.0 * ahead, jnp.where(col > row, ahead, behind))
    )
    row_high, row_low = halves(
        toeplitz(line(by_row, offset) + line(by_row, back), ROWS, OFFSETS)
    )
    around = toeplitz(line(by_col, offset) + line(by_col, back), 128, 0)
    inside = jnp.abs(col - row) < OFFSETS
    col_high, col_low = halves(
        jnp.concatenate([jnp.where(inside, around, 0.0), jnp.where(inside, 0.0, around)], axis=0)
    )

    nn = ((1,), (0,))
    zeros = jnp.zeros((128, 128), BF16)
    plane_left = jnp.concatenate(
        [
            jnp.concatenate([plane_high, plane_high], axis=1),
            jnp.concatenate([plane_low, zeros], axis=1),
        ],
        axis=0,
    )
    for part in range(ROWS // 8):
        values = field[:, 8 * part : 8 * part + 8, :].reshape(128, COLS)
        both = jnp.concatenate(halves(values), axis=0)
        product = contract(plane_left, both, nn)
        result[:, 8 * part : 8 * part + 8, :] = (product[:128] + product[128:]).reshape(
            PLANES, 8, COLS
        )

    row_left = jnp.concatenate([row_high, row_low], axis=0)
    block = iota((128, COLS), 1) // OFFSETS
    copies = []
    for group in range(GROUPS):
        values = field[2 * group : 2 * group + 2].reshape(128, COLS)
        halo = jnp.where(block == group, right[...], left[...])
        if group:
            halo = pltpu.roll(halo, 128 - OFFSETS * group, 1)
        high, low = halves(jnp.concatenate([values, halo], axis=1))
        total = contract(high, col_high, nn) + contract(high, col_low, nn)
        total = total + contract(low, col_high, nn)
        parts = []
        for plane in (2 * group, 2 * group + 1):
            tall = jnp.concatenate(
                [above[plane], field[plane], below[plane], jnp.zeros((32, COLS), F32)], axis=0
            )
            high, low = halves(tall)
            product = contract(row_left, high, nn)
            parts.append(product[:ROWS] + product[ROWS:] + contract(row_high, low, nn))
        total = total + jnp.concatenate(parts, axis=0)
        planes = slice(2 * group, 2 * group + 2)
        result[planes] = result[planes] + total.reshape(2, ROWS, COLS)
        copy = pltpu.make_async_copy(result.at[planes], gradient.at[planes], sems.at[group])
        copy.start()
        copies.append(copy)
    for copy in copies:
        copy.wait()


def shift(block, axes, forward):
    count = lax.axis_size(axes)
    step = 1 if forward else count - 1
    return lax.ppermute(block, axes, [(i, (i + step) % count) for i in range(count)])


def shaped(*shape):
    return jax.ShapeDtypeStruct(shape, F32)


def on_device(field, targets, weights):
    voxels = PLANES * ROWS * COLS * lax.axis_size(GY + GX)
    plane_count, line_count = lax.axis_size(PLANE), lax.axis_size(LINE)
    targets = jnp.pad(targets, ((0, 5), (0, 128 - OFFSETS)))
    weights = jnp.pad(weights, ((0, 5), (0, 128 - OFFSETS)))
    edge = shaped(PLANES, OFFSETS, COLS)
    side = shaped(128, COLS)
    top, bottom, first, last = pl.pallas_call(
        edges_kernel, out_shape=(edge, edge, side, side), name="edges"
    )(field)
    right = shift(first, GX, False)
    below = shift(top, GY, False)
    left = shift(last, GX, True)
    above = shift(bottom, GY, True)
    inner = pl.pallas_call(
        inner_kernel,
        out_shape=shaped(8, 128),
        name="inner",
        cost_estimate=pl.CostEstimate(flops=600_000_000, bytes_accessed=1 << 19, transcendentals=0),
    )(field)
    sums = pl.pallas_call(border_kernel, out_shape=shaped(plane_count, 8, 128), name="border")(
        inner, bottom, below, last, right
    )
    sums = lax.all_to_all(sums, PLANE, 0, 0).sum(0)
    totals = lax.all_to_all(
        jnp.broadcast_to(sums[None], (line_count, 8, 128)), LINE, 0, 0
    )
    vmem = pl.BlockSpec(memory_space=pltpu.VMEM)
    return pl.pallas_call(
        lambda *refs: gradient_kernel(voxels, *refs),
        out_shape=(shaped(PLANES, ROWS, COLS), shaped(3, OFFSETS)),
        in_specs=[vmem] * 8,
        out_specs=(HBM_SPEC, vmem),
        scratch_shapes=[
            pltpu.VMEM((PLANES, ROWS, COLS), F32),
            pltpu.SemaphoreType.DMA((GROUPS,)),
        ],
        name="gradient",
    )(field, above, below, left, right, totals, targets, weights)


def solution(mesh):
    devices = np.asarray(mesh.devices).reshape(4, 4, 2, 4, 4)
    fine = Mesh(devices, GY + GX)
    return jax.shard_map(
        on_device,
        mesh=fine,
        in_specs=(P(None, GY, GX), P(), P()),
        out_specs=(P(None, GY, GX), P()),
        check_vma=False,
    )
```

```python
import jax
import jax.numpy as jnp
import numpy as np
from jax import lax
from jax.experimental import pallas as pl
from jax.experimental.pallas import tpu as pltpu
from jax.sharding import Mesh, PartitionSpec as P

OFFSETS = 16
GY = ("zl", "y", "c")
GX = ("x", "zh")
PLANE = ("c", "y", "x")
LINE = ("zl", "zh")
PLANES, ROWS, COLS = 16, 64, 128
GROUPS = 8
F32, BF16 = jnp.float32, jnp.bfloat16
PAY = 8
INNER, BORDER = 600_000_000, 2_000_000_000
HBM_SPEC = pl.BlockSpec(memory_space=pl.ANY)


def iota(shape, dim):
    return lax.broadcasted_iota(jnp.int32, shape, dim)


def halves(values):
    high = values.astype(BF16)
    return high, (values - high.astype(F32)).astype(BF16)


def contract(left, right, dims):
    return lax.dot_general(left, right, (dims, ((), ())), preferred_element_type=F32)


def quadrants(gram):
    half = gram.shape[0] // 2
    tall = gram[:half] + gram[half:]
    return tall[:, :half] + tall[:, half:] if half == 128 else tall + pltpu.roll(tall, half, 1)


def diagonal_sums(gram, keep, base):
    gram = jnp.where(keep, gram, 0.0)
    total = jnp.zeros((8, 128), F32)
    for block in range(gram.shape[0] // 8):
        by = (base - 8 * block) % 128
        values = gram[8 * block : 8 * block + 8]
        total = total + (pltpu.roll(values, by, 1) if by else values)
    row = iota((8, 128), 0)
    for bit in (1, 2, 4):
        total = jnp.where(row & bit != 0, pltpu.roll(total, 128 - bit, 1), total)
    return jnp.sum(total, axis=0, keepdims=True)


def one_row(*sums):
    axis = iota((1, 128), 1) // OFFSETS
    row = jnp.where(axis == 0, sums[0], 0.0)
    for a in (1, 2):
        row = jnp.where(axis == a, pltpu.roll(sums[a], OFFSETS * a, 1), row)
    return row


def columns_kernel(field, first, last):
    block = iota((128, COLS), 1) // OFFSETS
    first_cols = jnp.zeros((128, COLS), F32)
    last_cols = jnp.zeros((128, COLS), F32)
    for group in range(GROUPS):
        values = field[2 * group : 2 * group + 2].reshape(128, COLS)
        moved = pltpu.roll(values, OFFSETS * group, 1) if group else values
        first_cols = jnp.where(block == group, moved, first_cols)
        last_cols = jnp.where(block == (group + 7) % 8, moved, last_cols)
    first[...] = first_cols
    last[...] = last_cols


def odd(axis):
    return lax.axis_index(axis) % 2 == 1


def swapped(flag, first, second):
    return jnp.where(flag, second, first), jnp.where(flag, first, second)


def rows_kernel(field, after, near_pair, far_pair):
    near_pair[...], far_pair[...] = swapped(
        odd("c"), field[:, ROWS - OFFSETS :, :], field[:, :OFFSETS, :]
    )


def again_kernel(first, after, out):
    out[...] = first[...]


def settle_kernel(right, after, out):
    out[...] = jnp.zeros_like(out)


def inner_kernel(field, out):
    gram = jnp.zeros((256, 256), F32)
    for part in range(ROWS // 8):
        values = field[:, 8 * part : 8 * part + 8, :].reshape(128, COLS)
        both = jnp.concatenate(halves(values), axis=0)
        gram = gram + contract(both, both, ((1,), (1,)))
    row, col = iota((128, 128), 0), iota((128, 128), 1)
    spread = diagonal_sums(quadrants(gram), (row % 8 == col % 8) & (col >= row), 0)
    gram = jnp.zeros((128, 128), F32)
    for plane in range(PLANES):
        both = jnp.concatenate(halves(field[plane]), axis=0)
        gram = gram + contract(both, both, ((1,), (1,)))
    apart = (col - row)[:ROWS]
    along_rows = diagonal_sums(quadrants(gram), (apart >= 0) & (apart < OFFSETS) & (col[:ROWS] < ROWS), 0)
    gram = jnp.zeros((256, 256), F32)
    for group in range(GROUPS):
        both = jnp.concatenate(halves(field[2 * group : 2 * group + 2].reshape(128, COLS)), axis=1)
        gram = gram + contract(both, both, ((0,), (0,)))
    apart = col - row
    along_cols = diagonal_sums(quadrants(gram), (apart >= 0) & (apart < OFFSETS), 0)
    lane, offset = iota((OFFSETS, 128), 1), iota((OFFSETS, 128), 0)
    column = jnp.sum(jnp.where(lane == 8 * offset, spread, 0.0), axis=1, keepdims=True)
    along_planes = jnp.sum(jnp.where(lane == offset, column, 0.0), axis=0, keepdims=True)
    out[...] = one_row(along_planes, along_rows, along_cols)


def border_cols_kernel(left, first, inner, out):
    row, col = iota((128, 128), 0), iota((128, 128), 1)
    mine = jnp.concatenate(halves(left[...]), axis=1)
    other = jnp.concatenate(halves(first[...]), axis=1)
    gram = quadrants(contract(mine, other, ((0,), (0,))))
    apart = (col - row + 128) % 128
    keep = ((row // 16 + 1) % 8 == col // 16) & (apart < OFFSETS) & (apart > 0)
    zeros = jnp.zeros((1, 128), F32)
    out[...] = inner[...] + one_row(zeros, zeros, diagonal_sums(gram, keep, 0))


def border_rows_kernel(mine_far, mine_near, row_far, row_near, sums, out):
    _, above = swapped(odd("c"), row_near[...], row_far[...])
    _, top = swapped(odd("c"), mine_near[...], mine_far[...])
    row, col = iota((128, 128), 0), iota((128, 128), 1)
    gram = jnp.zeros((128, 128), F32)
    for planes in (slice(0, 8), slice(8, 16)):
        mine_high, mine_low = halves(above[planes].reshape(128, COLS))
        next_high, next_low = halves(top[planes].reshape(128, COLS))
        product = contract(mine_high, jnp.concatenate([next_high, next_low], axis=0), ((1,), (1,)))
        gram = gram + product[:, :128] + product[:, 128:]
        gram = gram + contract(mine_low, next_high, ((1,), (1,)))
    zeros = jnp.zeros((1, 128), F32)
    along_rows = diagonal_sums(gram, (row // 16 == col // 16) & (col < row), OFFSETS)
    out[...] = jnp.broadcast_to((sums[...] + one_row(zeros, along_rows, zeros))[None], out.shape)


def gradient_kernel(
    voxels, field, row_far, row_near, left, right, totals, targets, weights, after, gradient, correlation, result, sems
):
    value = jnp.sum(totals[...], axis=0, keepdims=True) / jnp.float32(voxels)
    value = jnp.concatenate([value[:, OFFSETS * a : OFFSETS * (a + 1)] for a in range(3)], axis=0)
    correlation[...] = value
    coefficient = weights[...] * (value - targets[...])
    lane, offset = iota((OFFSETS, 128), 1), iota((OFFSETS, 128), 0)
    same = iota((OFFSETS, OFFSETS), 0) == iota((OFFSETS, OFFSETS), 1)

    def column(axis):
        return jnp.sum(
            jnp.where(same, coefficient[axis : axis + 1], 0.0), axis=1, keepdims=True
        )

    def line(values, lanes):
        return jnp.sum(jnp.where(lane == lanes, values, 0.0), axis=0, keepdims=True)

    def toeplitz(values, size, base):
        return pltpu.roll(
            jnp.broadcast_to(values, (size, 128)), base, 1, stride=1, stride_axis=0
        )

    def both(high, low):
        return jnp.concatenate(
            [
                jnp.concatenate([high, high], axis=1),
                jnp.concatenate([low, jnp.zeros_like(low)], axis=1),
            ],
            axis=0,
        )

    back = (128 - offset) % 128
    nn = ((1,), (0,))
    along_planes, along_rows, along_cols = column(0), column(1), column(2)
    row, col = iota((128, 128), 0), iota((128, 128), 1)
    around = toeplitz(line(along_cols, offset) + line(along_cols, back), 128, 0)
    inside = jnp.abs(col - row) < OFFSETS
    col_high, col_low = halves(
        jnp.concatenate([jnp.where(inside, around, 0.0), jnp.where(inside, 0.0, around)], axis=0)
    )
    row_left = both(
        *halves(
            toeplitz(line(along_rows, offset) + line(along_rows, back), ROWS, OFFSETS)[
                :, : ROWS + 32
            ]
        )
    )
    ahead = toeplitz(line(along_planes, 8 * offset), 128, 0)
    behind = toeplitz(line(along_planes, (128 - 8 * offset) % 128), 128, 0)
    plane_left = both(
        *halves(jnp.where(col == row, 2.0 * ahead, jnp.where(col > row, ahead, behind)))
    )
    below, above = swapped(odd("c"), row_near[...], row_far[...])

    for pair in range(ROWS // 16):
        parts = []
        for side in range(2):
            rows = slice(16 * pair + 8 * side, 16 * pair + 8 * side + 8)
            parts.append(jnp.concatenate(halves(field[:, rows, :].reshape(128, COLS)), axis=0))
        product = contract(plane_left, jnp.concatenate(parts, axis=1), nn)
        product = product[:128] + product[128:]
        for side in range(2):
            rows = slice(16 * pair + 8 * side, 16 * pair + 8 * side + 8)
            result[:, rows, :] = product[:, COLS * side : COLS * (side + 1)].reshape(PLANES, 8, COLS)

    block = iota((128, COLS), 1) // OFFSETS
    col_right = jnp.concatenate([col_high, col_low], axis=1)
    copies = []
    for group in range(GROUPS):
        values = field[2 * group : 2 * group + 2].reshape(128, COLS)
        halo = jnp.where(block == group, right[...], left[...])
        if group:
            halo = pltpu.roll(halo, 128 - OFFSETS * group, 1)
        high, low = halves(jnp.concatenate([values, halo], axis=1))
        product = contract(high, col_right, nn)
        total = product[:, :128] + product[:, 128:] + contract(low, col_high, nn)
        talls = []
        for plane in (2 * group, 2 * group + 1):
            tall = jnp.concatenate([above[plane], field[plane], below[plane]], axis=0)
            talls.append(jnp.concatenate(halves(tall), axis=0))
        product = contract(row_left, jnp.concatenate(talls, axis=1), nn)
        product = product[:ROWS] + product[ROWS:]
        total = total + jnp.concatenate([product[:, :COLS], product[:, COLS:]], axis=0)
        planes = slice(2 * group, 2 * group + 2)
        result[planes] = result[planes] + total.reshape(2, ROWS, COLS)
        copy = pltpu.make_async_copy(result.at[planes], gradient.at[planes], sems.at[group])
        copy.start()
        copies.append(copy)
    for copy in copies:
        copy.wait()


def middle_kernel(parts, out):
    total = jnp.sum(parts[...], axis=0)[:1]
    out[...] = jnp.broadcast_to(total, out.shape)


def shift(block, axes, forward):
    count = lax.axis_size(axes)
    step = 1 if forward else count - 1
    return lax.ppermute(block, axes, [(i, (i + step) % count) for i in range(count)])


def swap(block, axes, shift):
    count = lax.axis_size(axes)
    pairs = [(i, (i + 1) % count) for i in range(shift, count, 2)]
    return lax.ppermute(block, axes, [pair for i, j in pairs for pair in ((i, j), (j, i))])


def exchange(parts, axes):
    if parts.ndim == 2:
        return lax.all_to_all(parts[:, None], axes, 0, 0)[:, 0]
    return lax.all_to_all(parts, axes, 0, 0)


def resident(*shape):
    return pltpu.VMEM(shape, F32)


def near(values):
    return pltpu.with_memory_space_constraint(values, pltpu.VMEM)


def on_device(field, targets, weights):
    voxels = PLANES * ROWS * COLS * lax.axis_size(GY + GX)
    plane_count, line_count = lax.axis_size(PLANE), lax.axis_size(LINE)
    edge = resident(PLANES, OFFSETS, COLS)
    side = resident(128, COLS)
    vmem = pl.BlockSpec(memory_space=pltpu.VMEM)
    field = near(field)
    first, last = pl.pallas_call(
        columns_kernel,
        out_shape=(side, side),
        in_specs=[vmem],
        out_specs=(vmem,) * 2,
        name="columns",
    )(field)
    left = near(shift(last, GX, True))
    mine_near, mine_far = pl.pallas_call(
        rows_kernel, out_shape=(edge, edge), in_specs=[vmem] * 2, out_specs=(vmem,) * 2, name="rows"
    )(field, near(last))
    row_far = near(swap(mine_far, GY, 1))
    row_near = near(swap(mine_near, GY, 0))
    inner = pl.pallas_call(
        inner_kernel,
        out_shape=resident(1, 128),
        in_specs=[vmem],
        out_specs=vmem,
        name="inner",
        cost_estimate=pl.CostEstimate(flops=INNER, bytes_accessed=1 << 19, transcendentals=0),
    )(field)
    sums = pl.pallas_call(
        border_cols_kernel,
        out_shape=resident(1, 128),
        in_specs=[vmem] * 3,
        out_specs=vmem,
        name="border_cols",
        cost_estimate=pl.CostEstimate(flops=BORDER, bytes_accessed=1 << 17, transcendentals=0),
    )(left, near(first), near(inner))
    first_again = pl.pallas_call(
        again_kernel, out_shape=side, in_specs=[vmem] * 2, out_specs=vmem, name="again"
    )(near(first), near(sums))
    right = near(shift(first_again, GX, False))
    sums = pl.pallas_call(
        border_rows_kernel,
        out_shape=resident(plane_count, PAY, 128),
        in_specs=[vmem] * 5,
        out_specs=vmem,
        name="border_rows",
    )(near(mine_far), near(mine_near), row_far, row_near, near(sums))
    sums = pl.pallas_call(
        middle_kernel,
        out_shape=resident(line_count, 128),
        in_specs=[vmem],
        out_specs=vmem,
        name="middle",
    )(near(exchange(sums, PLANE)))
    totals = near(exchange(sums, LINE))
    settled = pl.pallas_call(
        settle_kernel, out_shape=resident(8, 128), in_specs=[vmem] * 2, out_specs=vmem, name="settle"
    )(right, near(sums))
    return pl.pallas_call(
        lambda *refs: gradient_kernel(voxels, *refs),
        out_shape=(jax.ShapeDtypeStruct((PLANES, ROWS, COLS), F32), jax.ShapeDtypeStruct((3, OFFSETS), F32)),
        in_specs=[vmem] * 9,
        out_specs=(HBM_SPEC, vmem),
        scratch_shapes=[
            pltpu.VMEM((PLANES, ROWS, COLS), F32),
            pltpu.SemaphoreType.DMA((GROUPS,)),
        ],
        name="gradient",
    )(field, row_far, row_near, left, right, totals, near(targets), near(weights), near(settled))


def solution(mesh):
    devices = np.asarray(mesh.devices).reshape(4, 4, 2, 4, 4)
    fine = Mesh(devices, GY + GX)
    return jax.shard_map(
        on_device,
        mesh=fine,
        in_specs=(P(None, GY, GX), P(), P()),
        out_specs=(P(None, GY, GX), P()),
        check_vma=False,
    )
```

```python
import jax
import jax.numpy as jnp
import numpy as np
from jax import lax
from jax.experimental import pallas as pl
from jax.experimental.pallas import tpu as pltpu
from jax.sharding import Mesh, PartitionSpec as P

OFFSETS = 16
GY = ("zl", "y", "c")
GX = ("x", "zh")
PLANE = ("c", "y", "x")
LINE = ("zl", "zh")
PLANES, ROWS, COLS = 16, 64, 128
GROUPS = 8
F32, BF16 = jnp.float32, jnp.bfloat16
PAY = 8
INNER, BORDER = 600_000_000, 2_000_000_000
HBM_SPEC = pl.BlockSpec(memory_space=pl.ANY)


def iota(shape, dim):
    return lax.broadcasted_iota(jnp.int32, shape, dim)


def halves(values):
    high = values.astype(BF16)
    return high, (values - high.astype(F32)).astype(BF16)


def contract(left, right, dims):
    return lax.dot_general(left, right, (dims, ((), ())), preferred_element_type=F32)


def quadrants(gram):
    half = gram.shape[0] // 2
    tall = gram[:half] + gram[half:]
    return tall[:, :half] + tall[:, half:] if half == 128 else tall + pltpu.roll(tall, half, 1)


def diagonal_sums(gram, keep, base):
    gram = jnp.where(keep, gram, 0.0)
    total = jnp.zeros((8, 128), F32)
    for block in range(gram.shape[0] // 8):
        by = (base - 8 * block) % 128
        values = gram[8 * block : 8 * block + 8]
        total = total + (pltpu.roll(values, by, 1) if by else values)
    row = iota((8, 128), 0)
    moved = jnp.where(row == 0, total, 0.0)
    for step in range(1, 8):
        moved = jnp.where(row == step, pltpu.roll(total, 128 - step, 1), moved)
    return jnp.sum(moved, axis=0, keepdims=True)


def lanes(axis):
    return OFFSETS * axis


def only(axis, sums):
    return jnp.where(iota((1, 128), 1) // OFFSETS == axis, sums, 0.0)


def odd(axis):
    return lax.axis_index(axis) % 2 == 1


def swapped(flag, first, second):
    return jnp.where(flag, second, first), jnp.where(flag, first, second)


def columns_kernel(field, early, late):
    block = iota((128, COLS), 1) // OFFSETS
    first = jnp.zeros((128, COLS), F32)
    last = jnp.zeros((128, COLS), F32)
    for group in range(GROUPS):
        values = field[2 * group : 2 * group + 2].reshape(128, COLS)
        moved = pltpu.roll(values, OFFSETS * group, 1) if group else values
        first = jnp.where(block == group, moved, first)
        last = jnp.where(block == (group + 7) % 8, moved, last)
    early[...], late[...] = swapped(odd("c"), last, first)


def rows_kernel(field, after, near_pair, far_pair):
    near_pair[...], far_pair[...] = swapped(
        odd("c"), field[:, ROWS - OFFSETS :, :], field[:, :OFFSETS, :]
    )


def again_kernel(late, after, out):
    out[...] = late[...]


def inner_kernel(field, out):
    gram = jnp.zeros((256, 256), F32)
    for part in range(ROWS // 8):
        values = field[:, 8 * part : 8 * part + 8, :].reshape(128, COLS)
        both = jnp.concatenate(halves(values), axis=0)
        gram = gram + contract(both, both, ((1,), (1,)))
    row, col = iota((128, 128), 0), iota((128, 128), 1)
    spread = diagonal_sums(quadrants(gram), (row % 8 == col % 8) & (col >= row), 0)
    gram = jnp.zeros((128, 128), F32)
    for plane in range(PLANES):
        both = jnp.concatenate(halves(field[plane]), axis=0)
        gram = gram + contract(both, both, ((1,), (1,)))
    apart = (col - row)[:ROWS]
    along_rows = diagonal_sums(
        quadrants(gram), (apart >= 0) & (apart < OFFSETS) & (col[:ROWS] < ROWS), lanes(1)
    )
    gram = jnp.zeros((256, 256), F32)
    for group in range(GROUPS):
        both = jnp.concatenate(halves(field[2 * group : 2 * group + 2].reshape(128, COLS)), axis=1)
        gram = gram + contract(both, both, ((0,), (0,)))
    apart = col - row
    along_cols = diagonal_sums(quadrants(gram), (apart >= 0) & (apart < OFFSETS), lanes(2))
    lane, offset = iota((OFFSETS, 128), 1), iota((OFFSETS, 128), 0)
    column = jnp.sum(jnp.where(lane == 8 * offset, spread, 0.0), axis=1, keepdims=True)
    along_planes = jnp.sum(jnp.where(lane == offset, column, 0.0), axis=0, keepdims=True)
    out[...] = only(0, along_planes) + only(1, along_rows) + only(2, along_cols)


def border_cols_kernel(received, late, inner, out):
    left, right = swapped(odd("c"), received[...], late[...])
    row, col = iota((128, 128), 0), iota((128, 128), 1)
    mine = jnp.concatenate(halves(left), axis=1)
    other = jnp.concatenate(halves(right), axis=1)
    gram = quadrants(contract(mine, other, ((0,), (0,))))
    apart = (col - row + 128) % 128
    keep = ((row // 16 + 1) % 8 == col // 16) & (apart < OFFSETS) & (apart > 0)
    out[...] = inner[...] + only(2, diagonal_sums(gram, keep, lanes(2)))


def border_rows_kernel(mine_far, mine_near, row_far, row_near, sums, out):
    _, above = swapped(odd("c"), row_near[...], row_far[...])
    _, top = swapped(odd("c"), mine_near[...], mine_far[...])
    row, col = iota((128, 128), 0), iota((128, 128), 1)
    gram = jnp.zeros((128, 128), F32)
    for planes in (slice(0, 8), slice(8, 16)):
        mine_high, mine_low = halves(above[planes].reshape(128, COLS))
        next_high, next_low = halves(top[planes].reshape(128, COLS))
        product = contract(mine_high, jnp.concatenate([next_high, next_low], axis=0), ((1,), (1,)))
        gram = gram + product[:, :128] + product[:, 128:]
        gram = gram + contract(mine_low, next_high, ((1,), (1,)))
    along_rows = diagonal_sums(gram, (row // 16 == col // 16) & (col < row), OFFSETS + lanes(1))
    out[...] = jnp.broadcast_to((sums[...] + only(1, along_rows))[None], out.shape)


def gradient_kernel(
    voxels, field, row_far, row_near, col_early, col_late, totals, targets, weights, gradient, correlation, result, value_ref, sems
):
    value = jnp.sum(totals[...], axis=0, keepdims=True) / jnp.float32(voxels)
    value = jnp.concatenate([value[:, OFFSETS * a : OFFSETS * (a + 1)] for a in range(3)], axis=0)
    value_ref[...] = value
    copies = [pltpu.make_async_copy(value_ref, correlation, sems.at[GROUPS])]
    copies[0].start()
    coefficient = weights[...] * (value - targets[...])
    lane, offset = iota((OFFSETS, 128), 1), iota((OFFSETS, 128), 0)
    same = iota((OFFSETS, OFFSETS), 0) == iota((OFFSETS, OFFSETS), 1)

    def column(axis):
        return jnp.sum(
            jnp.where(same, coefficient[axis : axis + 1], 0.0), axis=1, keepdims=True
        )

    def line(values, lanes):
        return jnp.sum(jnp.where(lane == lanes, values, 0.0), axis=0, keepdims=True)

    def toeplitz(values, size, base):
        return pltpu.roll(
            jnp.broadcast_to(values, (size, 128)), base, 1, stride=1, stride_axis=0
        )

    def both(high, low):
        return jnp.concatenate(
            [
                jnp.concatenate([high, high], axis=1),
                jnp.concatenate([low, jnp.zeros_like(low)], axis=1),
            ],
            axis=0,
        )

    back = (128 - offset) % 128
    nn = ((1,), (0,))
    along_planes, along_rows, along_cols = column(0), column(1), column(2)
    row, col = iota((128, 128), 0), iota((128, 128), 1)
    around = toeplitz(line(along_cols, offset) + line(along_cols, back), 128, 0)
    inside = jnp.abs(col - row) < OFFSETS
    col_high, col_low = halves(
        jnp.concatenate([jnp.where(inside, around, 0.0), jnp.where(inside, 0.0, around)], axis=0)
    )
    row_left = both(
        *halves(
            toeplitz(line(along_rows, offset) + line(along_rows, back), ROWS, OFFSETS)[
                :, : ROWS + 32
            ]
        )
    )
    ahead = toeplitz(line(along_planes, 8 * offset), 128, 0)
    behind = toeplitz(line(along_planes, (128 - 8 * offset) % 128), 128, 0)
    plane_left = both(
        *halves(jnp.where(col == row, 2.0 * ahead, jnp.where(col > row, ahead, behind)))
    )
    below, above = swapped(odd("c"), row_near[...], row_far[...])
    left, right = swapped(odd("c"), col_early[...], col_late[...])

    for pair in range(ROWS // 16):
        parts = []
        for side in range(2):
            rows = slice(16 * pair + 8 * side, 16 * pair + 8 * side + 8)
            parts.append(jnp.concatenate(halves(field[:, rows, :].reshape(128, COLS)), axis=0))
        product = contract(plane_left, jnp.concatenate(parts, axis=1), nn)
        product = product[:128] + product[128:]
        for side in range(2):
            rows = slice(16 * pair + 8 * side, 16 * pair + 8 * side + 8)
            result[:, rows, :] = product[:, COLS * side : COLS * (side + 1)].reshape(PLANES, 8, COLS)

    block = iota((128, COLS), 1) // OFFSETS
    col_right = jnp.concatenate([col_high, col_low], axis=1)
    for group in range(GROUPS):
        values = field[2 * group : 2 * group + 2].reshape(128, COLS)
        halo = jnp.where(block == group, right, left)
        if group:
            halo = pltpu.roll(halo, 128 - OFFSETS * group, 1)
        high, low = halves(jnp.concatenate([values, halo], axis=1))
        product = contract(high, col_right, nn)
        total = product[:, :128] + product[:, 128:] + contract(low, col_high, nn)
        talls = []
        for plane in (2 * group, 2 * group + 1):
            tall = jnp.concatenate([above[plane], field[plane], below[plane]], axis=0)
            talls.append(jnp.concatenate(halves(tall), axis=0))
        product = contract(row_left, jnp.concatenate(talls, axis=1), nn)
        product = product[:ROWS] + product[ROWS:]
        total = total + jnp.concatenate([product[:, :COLS], product[:, COLS:]], axis=0)
        planes = slice(2 * group, 2 * group + 2)
        result[planes] = result[planes] + total.reshape(2, ROWS, COLS)
        copy = pltpu.make_async_copy(result.at[planes], gradient.at[planes], sems.at[group])
        copy.start()
        copies.append(copy)
    for copy in copies:
        copy.wait()


def middle_kernel(parts, out):
    total = jnp.sum(parts[...], axis=0)[:1]
    out[...] = jnp.broadcast_to(total, out.shape)


def pass_on(block, early):
    rows, cols = lax.axis_size(GY), lax.axis_size(GX)
    pairs = []
    for row in range(rows):
        step = 1 if (row % 2 == 0) == early else cols - 1
        pairs += [(row * cols + i, row * cols + (i + step) % cols) for i in range(cols)]
    return lax.ppermute(block, GY + GX, pairs)


def swap(block, axes, shift):
    count = lax.axis_size(axes)
    pairs = [(i, (i + 1) % count) for i in range(shift, count, 2)]
    return lax.ppermute(block, axes, [pair for i, j in pairs for pair in ((i, j), (j, i))])


def exchange(parts, axes):
    if parts.ndim == 2:
        return lax.all_to_all(parts[:, None], axes, 0, 0)[:, 0]
    return lax.all_to_all(parts, axes, 0, 0)


def resident(*shape):
    return pltpu.VMEM(shape, F32)


def near(values):
    return pltpu.with_memory_space_constraint(values, pltpu.VMEM)


def on_device(field, targets, weights):
    voxels = PLANES * ROWS * COLS * lax.axis_size(GY + GX)
    plane_count, line_count = lax.axis_size(PLANE), lax.axis_size(LINE)
    edge = resident(PLANES, OFFSETS, COLS)
    side = resident(128, COLS)
    vmem = pl.BlockSpec(memory_space=pltpu.VMEM)
    field = near(field)
    early, late = pl.pallas_call(
        columns_kernel,
        out_shape=(side, side),
        in_specs=[vmem],
        out_specs=(vmem,) * 2,
        name="columns",
    )(field)
    col_early = near(pass_on(early, True))
    mine_near, mine_far = pl.pallas_call(
        rows_kernel, out_shape=(edge, edge), in_specs=[vmem] * 2, out_specs=(vmem,) * 2, name="rows"
    )(field, near(early))
    row_far = near(swap(mine_far, GY, 1))
    row_near = near(swap(mine_near, GY, 0))
    inner = pl.pallas_call(
        inner_kernel,
        out_shape=resident(1, 128),
        in_specs=[vmem],
        out_specs=vmem,
        name="inner",
        cost_estimate=pl.CostEstimate(flops=INNER, bytes_accessed=1 << 19, transcendentals=0),
    )(field)
    sums = pl.pallas_call(
        border_cols_kernel,
        out_shape=resident(1, 128),
        in_specs=[vmem] * 3,
        out_specs=vmem,
        name="border_cols",
        cost_estimate=pl.CostEstimate(flops=BORDER, bytes_accessed=1 << 17, transcendentals=0),
    )(col_early, near(late), near(inner))
    late_again = pl.pallas_call(
        again_kernel, out_shape=side, in_specs=[vmem] * 2, out_specs=vmem, name="again"
    )(near(late), near(sums))
    col_late = near(pass_on(late_again, False))
    sums = pl.pallas_call(
        border_rows_kernel,
        out_shape=resident(plane_count, PAY, 128),
        in_specs=[vmem] * 5,
        out_specs=vmem,
        name="border_rows",
    )(near(mine_far), near(mine_near), row_far, row_near, near(sums))
    sums = pl.pallas_call(
        middle_kernel,
        out_shape=resident(line_count, 128),
        in_specs=[vmem],
        out_specs=vmem,
        name="middle",
    )(near(exchange(sums, PLANE)))
    totals = near(exchange(sums, LINE))
    return pl.pallas_call(
        lambda *refs: gradient_kernel(voxels, *refs),
        out_shape=(jax.ShapeDtypeStruct((PLANES, ROWS, COLS), F32), jax.ShapeDtypeStruct((3, OFFSETS), F32)),
        in_specs=[vmem] * 8,
        out_specs=(HBM_SPEC, HBM_SPEC),
        scratch_shapes=[
            pltpu.VMEM((PLANES, ROWS, COLS), F32),
            pltpu.VMEM((3, OFFSETS), F32),
            pltpu.SemaphoreType.DMA((GROUPS + 1,)),
        ],
        name="gradient",
    )(field, row_far, row_near, col_early, col_late, totals, near(targets), near(weights))


def solution(mesh):
    devices = np.asarray(mesh.devices).reshape(4, 4, 2, 4, 4)
    fine = Mesh(devices, GY + GX)
    return jax.shard_map(
        on_device,
        mesh=fine,
        in_specs=(P(None, GY, GX), P(), P()),
        out_specs=(P(None, GY, GX), P()),
        check_vma=False,
    )
```

```python
import jax
import jax.numpy as jnp
import numpy as np
from jax import lax
from jax.experimental import pallas as pl
from jax.experimental.pallas import tpu as pltpu
from jax.sharding import Mesh, PartitionSpec as P

OFFSETS = 16
GY = ("zl", "y", "c")
GX = ("x", "zh")
PLANE = ("c", "y", "x")
LINE = ("zl", "zh")
PLANES, ROWS, COLS = 16, 64, 128
GROUPS = 8
F32, BF16 = jnp.float32, jnp.bfloat16
PAY = 2
MIDDLE = 300_000_000
INNER, BORDER = 600_000_000, 2_000_000_000
HBM_SPEC = pl.BlockSpec(memory_space=pl.ANY)


def iota(shape, dim):
    return lax.broadcasted_iota(jnp.int32, shape, dim)


def halves(values):
    high = values.astype(BF16)
    return high, (values - high.astype(F32)).astype(BF16)


def contract(left, right, dims):
    return lax.dot_general(left, right, (dims, ((), ())), preferred_element_type=F32)


def quadrants(gram):
    half = gram.shape[0] // 2
    tall = gram[:half] + gram[half:]
    return tall[:, :half] + tall[:, half:] if half == 128 else tall + pltpu.roll(tall, half, 1)


def diagonal_sums(gram, keep, base):
    gram = jnp.where(keep, gram, 0.0)
    total = jnp.zeros((8, 128), F32)
    for block in range(gram.shape[0] // 8):
        by = (base - 8 * block) % 128
        values = gram[8 * block : 8 * block + 8]
        total = total + (pltpu.roll(values, by, 1) if by else values)
    row = iota((8, 128), 0)
    moved = jnp.where(row == 0, total, 0.0)
    for step in range(1, 8):
        moved = jnp.where(row == step, pltpu.roll(total, 128 - step, 1), moved)
    return jnp.sum(moved, axis=0, keepdims=True)


def lanes(axis):
    return OFFSETS * axis


def only(axis, sums):
    return jnp.where(iota((1, 128), 1) // OFFSETS == axis, sums, 0.0)


def odd(axis):
    return lax.axis_index(axis) % 2 == 1


def swapped(flag, first, second):
    return jnp.where(flag, second, first), jnp.where(flag, first, second)


def columns_kernel(field, early, late):
    block = iota((128, COLS), 1) // OFFSETS
    first = jnp.zeros((128, COLS), F32)
    last = jnp.zeros((128, COLS), F32)
    for group in range(GROUPS):
        values = field[2 * group : 2 * group + 2].reshape(128, COLS)
        moved = pltpu.roll(values, OFFSETS * group, 1) if group else values
        first = jnp.where(block == group, moved, first)
        last = jnp.where(block == (group + 7) % 8, moved, last)
    early[...], late[...] = swapped(odd("c"), last, first)


def rows_kernel(field, after, near_pair, far_pair):
    near_pair[...], far_pair[...] = swapped(
        odd("c"), field[:, ROWS - OFFSETS :, :], field[:, :OFFSETS, :]
    )


def again_kernel(late, after, out):
    out[...] = late[...]


def inner_kernel(field, out):
    gram = jnp.zeros((256, 256), F32)
    for part in range(ROWS // 8):
        values = field[:, 8 * part : 8 * part + 8, :].reshape(128, COLS)
        both = jnp.concatenate(halves(values), axis=0)
        gram = gram + contract(both, both, ((1,), (1,)))
    row, col = iota((128, 128), 0), iota((128, 128), 1)
    spread = diagonal_sums(quadrants(gram), (row % 8 == col % 8) & (col >= row), 0)
    gram = jnp.zeros((128, 128), F32)
    for plane in range(PLANES):
        both = jnp.concatenate(halves(field[plane]), axis=0)
        gram = gram + contract(both, both, ((1,), (1,)))
    apart = (col - row)[:ROWS]
    along_rows = diagonal_sums(
        quadrants(gram), (apart >= 0) & (apart < OFFSETS) & (col[:ROWS] < ROWS), lanes(1)
    )
    gram = jnp.zeros((256, 256), F32)
    for group in range(GROUPS):
        both = jnp.concatenate(halves(field[2 * group : 2 * group + 2].reshape(128, COLS)), axis=1)
        gram = gram + contract(both, both, ((0,), (0,)))
    apart = col - row
    along_cols = diagonal_sums(quadrants(gram), (apart >= 0) & (apart < OFFSETS), lanes(2))
    lane, offset = iota((OFFSETS, 128), 1), iota((OFFSETS, 128), 0)
    column = jnp.sum(jnp.where(lane == 8 * offset, spread, 0.0), axis=1, keepdims=True)
    along_planes = jnp.sum(jnp.where(lane == offset, column, 0.0), axis=0, keepdims=True)
    out[...] = only(0, along_planes) + only(1, along_rows) + only(2, along_cols)


def border_cols_kernel(received, late, inner, out):
    left, right = swapped(odd("c"), received[...], late[...])
    row, col = iota((128, 128), 0), iota((128, 128), 1)
    mine = jnp.concatenate(halves(left), axis=1)
    other = jnp.concatenate(halves(right), axis=1)
    gram = quadrants(contract(mine, other, ((0,), (0,))))
    apart = (col - row + 128) % 128
    keep = ((row // 16 + 1) % 8 == col // 16) & (apart < OFFSETS) & (apart > 0)
    out[...] = inner[...] + only(2, diagonal_sums(gram, keep, lanes(2)))


def border_rows_kernel(mine_far, mine_near, row_far, row_near, sums, out):
    _, above = swapped(odd("c"), row_near[...], row_far[...])
    _, top = swapped(odd("c"), mine_near[...], mine_far[...])
    row, col = iota((128, 128), 0), iota((128, 128), 1)
    gram = jnp.zeros((128, 128), F32)
    for planes in (slice(0, 8), slice(8, 16)):
        mine_high, mine_low = halves(above[planes].reshape(128, COLS))
        next_high, next_low = halves(top[planes].reshape(128, COLS))
        product = contract(mine_high, jnp.concatenate([next_high, next_low], axis=0), ((1,), (1,)))
        gram = gram + product[:, :128] + product[:, 128:]
        gram = gram + contract(mine_low, next_high, ((1,), (1,)))
    along_rows = diagonal_sums(gram, (row // 16 == col // 16) & (col < row), OFFSETS + lanes(1))
    out[...] = jnp.broadcast_to((sums[...] + only(1, along_rows))[None], out.shape)


def gradient_kernel(
    voxels, field, row_far, row_near, col_early, col_late, totals, targets, weights, gradient, correlation, result, value_ref, sems
):
    value = jnp.sum(totals[...], axis=0, keepdims=True) / jnp.float32(voxels)
    value = jnp.concatenate([value[:, OFFSETS * a : OFFSETS * (a + 1)] for a in range(3)], axis=0)
    value_ref[...] = value
    copies = [pltpu.make_async_copy(value_ref, correlation, sems.at[GROUPS])]
    copies[0].start()
    coefficient = weights[...] * (value - targets[...])
    lane, offset = iota((OFFSETS, 128), 1), iota((OFFSETS, 128), 0)
    same = iota((OFFSETS, OFFSETS), 0) == iota((OFFSETS, OFFSETS), 1)

    def column(axis):
        return jnp.sum(
            jnp.where(same, coefficient[axis : axis + 1], 0.0), axis=1, keepdims=True
        )

    def line(values, lanes):
        return jnp.sum(jnp.where(lane == lanes, values, 0.0), axis=0, keepdims=True)

    def toeplitz(values, size, base):
        return pltpu.roll(
            jnp.broadcast_to(values, (size, 128)), base, 1, stride=1, stride_axis=0
        )

    def both(high, low):
        return jnp.concatenate(
            [
                jnp.concatenate([high, high], axis=1),
                jnp.concatenate([low, jnp.zeros_like(low)], axis=1),
            ],
            axis=0,
        )

    back = (128 - offset) % 128
    nn = ((1,), (0,))
    along_planes, along_rows, along_cols = column(0), column(1), column(2)
    row, col = iota((128, 128), 0), iota((128, 128), 1)
    around = toeplitz(line(along_cols, offset) + line(along_cols, back), 128, 0)
    inside = jnp.abs(col - row) < OFFSETS
    col_high, col_low = halves(
        jnp.concatenate([jnp.where(inside, around, 0.0), jnp.where(inside, 0.0, around)], axis=0)
    )
    row_left = both(
        *halves(
            toeplitz(line(along_rows, offset) + line(along_rows, back), ROWS, OFFSETS)[
                :, : ROWS + 32
            ]
        )
    )
    ahead = toeplitz(line(along_planes, 8 * offset), 128, 0)
    behind = toeplitz(line(along_planes, (128 - 8 * offset) % 128), 128, 0)
    plane_left = both(
        *halves(jnp.where(col == row, 2.0 * ahead, jnp.where(col > row, ahead, behind)))
    )
    below, above = swapped(odd("c"), row_near[...], row_far[...])
    left, right = swapped(odd("c"), col_early[...], col_late[...])

    for pair in range(ROWS // 16):
        parts = []
        for side in range(2):
            rows = slice(16 * pair + 8 * side, 16 * pair + 8 * side + 8)
            parts.append(jnp.concatenate(halves(field[:, rows, :].reshape(128, COLS)), axis=0))
        product = contract(plane_left, jnp.concatenate(parts, axis=1), nn)
        product = product[:128] + product[128:]
        for side in range(2):
            rows = slice(16 * pair + 8 * side, 16 * pair + 8 * side + 8)
            result[:, rows, :] = product[:, COLS * side : COLS * (side + 1)].reshape(PLANES, 8, COLS)

    block = iota((128, COLS), 1) // OFFSETS
    col_right = jnp.concatenate([col_high, col_low], axis=1)
    for group in range(GROUPS):
        values = field[2 * group : 2 * group + 2].reshape(128, COLS)
        halo = jnp.where(block == group, right, left)
        if group:
            halo = pltpu.roll(halo, 128 - OFFSETS * group, 1)
        high, low = halves(jnp.concatenate([values, halo], axis=1))
        product = contract(high, col_right, nn)
        total = product[:, :128] + product[:, 128:] + contract(low, col_high, nn)
        talls = []
        for plane in (2 * group, 2 * group + 1):
            tall = jnp.concatenate([above[plane], field[plane], below[plane]], axis=0)
            talls.append(jnp.concatenate(halves(tall), axis=0))
        product = contract(row_left, jnp.concatenate(talls, axis=1), nn)
        product = product[:ROWS] + product[ROWS:]
        total = total + jnp.concatenate([product[:, :COLS], product[:, COLS:]], axis=0)
        planes = slice(2 * group, 2 * group + 2)
        result[planes] = result[planes] + total.reshape(2, ROWS, COLS)
        copy = pltpu.make_async_copy(result.at[planes], gradient.at[planes], sems.at[group])
        copy.start()
        copies.append(copy)
    for copy in copies:
        copy.wait()


def middle_kernel(parts, out):
    total = jnp.sum(parts[...], axis=0)[:1]
    out[...] = jnp.broadcast_to(total, out.shape)


def pass_on(block, early):
    rows, cols = lax.axis_size(GY), lax.axis_size(GX)
    pairs = []
    for row in range(rows):
        step = 1 if (row % 2 == 0) == early else cols - 1
        pairs += [(row * cols + i, row * cols + (i + step) % cols) for i in range(cols)]
    return lax.ppermute(block, GY + GX, pairs)


def swap(block, axes, shift):
    count = lax.axis_size(axes)
    pairs = [(i, (i + 1) % count) for i in range(shift, count, 2)]
    return lax.ppermute(block, axes, [pair for i, j in pairs for pair in ((i, j), (j, i))])


def settle_kernel(sums, after, out):
    out[...] = sums[...]


def exchange(parts, axes):
    if parts.ndim == 2:
        return lax.all_to_all(parts[:, None], axes, 0, 0)[:, 0]
    return lax.all_to_all(parts, axes, 0, 0)


def resident(*shape):
    return pltpu.VMEM(shape, F32)


def near(values):
    return pltpu.with_memory_space_constraint(values, pltpu.VMEM)


def on_device(field, targets, weights):
    voxels = PLANES * ROWS * COLS * lax.axis_size(GY + GX)
    plane_count, line_count = lax.axis_size(PLANE), lax.axis_size(LINE)
    edge = resident(PLANES, OFFSETS, COLS)
    side = resident(128, COLS)
    vmem = pl.BlockSpec(memory_space=pltpu.VMEM)
    field = near(field)
    early, late = pl.pallas_call(
        columns_kernel,
        out_shape=(side, side),
        in_specs=[vmem],
        out_specs=(vmem,) * 2,
        name="columns",
    )(field)
    col_early = near(pass_on(early, True))
    mine_near, mine_far = pl.pallas_call(
        rows_kernel, out_shape=(edge, edge), in_specs=[vmem] * 2, out_specs=(vmem,) * 2, name="rows"
    )(field, near(early))
    row_far = near(swap(mine_far, GY, 1))
    row_near = near(swap(mine_near, GY, 0))
    inner = pl.pallas_call(
        inner_kernel,
        out_shape=resident(1, 128),
        in_specs=[vmem],
        out_specs=vmem,
        name="inner",
        cost_estimate=pl.CostEstimate(flops=INNER, bytes_accessed=1 << 19, transcendentals=0),
    )(field)
    sums = pl.pallas_call(
        border_cols_kernel,
        out_shape=resident(1, 128),
        in_specs=[vmem] * 3,
        out_specs=vmem,
        name="border_cols",
        cost_estimate=pl.CostEstimate(flops=BORDER, bytes_accessed=1 << 17, transcendentals=0),
    )(col_early, near(late), near(inner))
    late_again = pl.pallas_call(
        again_kernel, out_shape=side, in_specs=[vmem] * 2, out_specs=vmem, name="again"
    )(near(late), near(sums))
    col_late = near(pass_on(late_again, False))
    sums = pl.pallas_call(
        border_rows_kernel,
        out_shape=resident(line_count, PAY, 128),
        in_specs=[vmem] * 5,
        out_specs=vmem,
        name="border_rows",
    )(near(mine_far), near(mine_near), row_far, row_near, near(sums))
    sums = pl.pallas_call(
        middle_kernel,
        out_shape=resident(plane_count, 128),
        in_specs=[vmem],
        out_specs=vmem,
        name="middle",
        cost_estimate=pl.CostEstimate(flops=MIDDLE, bytes_accessed=1 << 14, transcendentals=0),
    )(near(exchange(sums, LINE)))
    sums = pl.pallas_call(
        settle_kernel,
        out_shape=resident(plane_count, 128),
        in_specs=[vmem] * 2,
        out_specs=vmem,
        name="settle",
    )(near(sums), col_late)
    totals = near(exchange(sums, PLANE))
    return pl.pallas_call(
        lambda *refs: gradient_kernel(voxels, *refs),
        out_shape=(jax.ShapeDtypeStruct((PLANES, ROWS, COLS), F32), jax.ShapeDtypeStruct((3, OFFSETS), F32)),
        in_specs=[vmem] * 8,
        out_specs=(HBM_SPEC, HBM_SPEC),
        scratch_shapes=[
            pltpu.VMEM((PLANES, ROWS, COLS), F32),
            pltpu.VMEM((3, OFFSETS), F32),
            pltpu.SemaphoreType.DMA((GROUPS + 1,)),
        ],
        name="gradient",
    )(field, row_far, row_near, col_early, col_late, totals, near(targets), near(weights))


def solution(mesh):
    devices = np.asarray(mesh.devices).reshape(4, 4, 2, 4, 4)
    fine = Mesh(devices, GY + GX)
    return jax.shard_map(
        on_device,
        mesh=fine,
        in_specs=(P(None, GY, GX), P(), P()),
        out_specs=(P(None, GY, GX), P()),
        check_vma=False,
    )
```

```python
import jax
import jax.numpy as jnp
import numpy as np
from jax import lax
from jax.experimental import pallas as pl
from jax.experimental.pallas import tpu as pltpu
from jax.sharding import Mesh, PartitionSpec as P

OFFSETS = 16
GY = ("zl", "y", "c")
GX = ("x", "zh")
PLANE = ("c", "y", "x")
LINE = ("zl", "zh")
PLANES, ROWS, COLS = 16, 64, 128
GROUPS = 8
F32, BF16 = jnp.float32, jnp.bfloat16
PAY = 2
MIDDLE = 300_000_000
INNER, BORDER = 600_000_000, 2_000_000_000
HBM_SPEC = pl.BlockSpec(memory_space=pl.ANY)


def iota(shape, dim):
    return lax.broadcasted_iota(jnp.int32, shape, dim)


def halves(values):
    high = values.astype(BF16)
    return high, (values - high.astype(F32)).astype(BF16)


def contract(left, right, dims):
    return lax.dot_general(left, right, (dims, ((), ())), preferred_element_type=F32)


def quadrants(gram):
    half = gram.shape[0] // 2
    tall = gram[:half] + gram[half:]
    return tall[:, :half] + tall[:, half:] if half == 128 else tall + pltpu.roll(tall, half, 1)


def diagonal_sums(gram, keep, base):
    gram = jnp.where(keep, gram, 0.0)
    total = jnp.zeros((8, 128), F32)
    for block in range(gram.shape[0] // 8):
        by = (base - 8 * block) % 128
        values = gram[8 * block : 8 * block + 8]
        total = total + (pltpu.roll(values, by, 1) if by else values)
    row = iota((8, 128), 0)
    moved = jnp.where(row == 0, total, 0.0)
    for step in range(1, 8):
        moved = jnp.where(row == step, pltpu.roll(total, 128 - step, 1), moved)
    return jnp.sum(moved, axis=0, keepdims=True)


def lanes(axis):
    return OFFSETS * axis


def only(axis, sums):
    return jnp.where(iota((1, 128), 1) // OFFSETS == axis, sums, 0.0)


def odd(axis):
    return lax.axis_index(axis) % 2 == 1


def swapped(flag, first, second):
    return jnp.where(flag, second, first), jnp.where(flag, first, second)


def columns_kernel(field, early, late):
    block = iota((128, COLS), 1) // OFFSETS
    first = jnp.zeros((128, COLS), F32)
    last = jnp.zeros((128, COLS), F32)
    for group in range(GROUPS):
        values = field[2 * group : 2 * group + 2].reshape(128, COLS)
        moved = pltpu.roll(values, OFFSETS * group, 1) if group else values
        first = jnp.where(block == group, moved, first)
        last = jnp.where(block == (group + 7) % 8, moved, last)
    early[...], late[...] = swapped(odd("c"), last, first)


def rows_kernel(field, after, near_pair, far_pair):
    near_pair[...], far_pair[...] = swapped(
        odd("c"), field[:, ROWS - OFFSETS :, :], field[:, :OFFSETS, :]
    )


def again_kernel(late, after, out):
    out[...] = late[...]


def inner_kernel(field, out):
    gram = jnp.zeros((256, 256), F32)
    for part in range(ROWS // 8):
        values = field[:, 8 * part : 8 * part + 8, :].reshape(128, COLS)
        both = jnp.concatenate(halves(values), axis=0)
        gram = gram + contract(both, both, ((1,), (1,)))
    row, col = iota((128, 128), 0), iota((128, 128), 1)
    spread = diagonal_sums(quadrants(gram), (row % 8 == col % 8) & (col >= row), 0)
    gram = jnp.zeros((128, 128), F32)
    for plane in range(PLANES):
        both = jnp.concatenate(halves(field[plane]), axis=0)
        gram = gram + contract(both, both, ((1,), (1,)))
    apart = (col - row)[:ROWS]
    along_rows = diagonal_sums(
        quadrants(gram), (apart >= 0) & (apart < OFFSETS) & (col[:ROWS] < ROWS), lanes(1)
    )
    gram = jnp.zeros((256, 256), F32)
    for group in range(GROUPS):
        both = jnp.concatenate(halves(field[2 * group : 2 * group + 2].reshape(128, COLS)), axis=1)
        gram = gram + contract(both, both, ((0,), (0,)))
    apart = col - row
    along_cols = diagonal_sums(quadrants(gram), (apart >= 0) & (apart < OFFSETS), lanes(2))
    lane, offset = iota((OFFSETS, 128), 1), iota((OFFSETS, 128), 0)
    column = jnp.sum(jnp.where(lane == 8 * offset, spread, 0.0), axis=1, keepdims=True)
    along_planes = jnp.sum(jnp.where(lane == offset, column, 0.0), axis=0, keepdims=True)
    out[...] = only(0, along_planes) + only(1, along_rows) + only(2, along_cols)


def border_cols_kernel(received, late, inner, out):
    left, right = swapped(odd("c"), received[...], late[...])
    row, col = iota((128, 128), 0), iota((128, 128), 1)
    mine = jnp.concatenate(halves(left), axis=1)
    other = jnp.concatenate(halves(right), axis=1)
    gram = quadrants(contract(mine, other, ((0,), (0,))))
    apart = (col - row + 128) % 128
    keep = ((row // 16 + 1) % 8 == col // 16) & (apart < OFFSETS) & (apart > 0)
    out[...] = inner[...] + only(2, diagonal_sums(gram, keep, lanes(2)))


def border_rows_kernel(mine_far, mine_near, row_far, row_near, sums, out):
    _, above = swapped(odd("c"), row_near[...], row_far[...])
    _, top = swapped(odd("c"), mine_near[...], mine_far[...])
    row, col = iota((128, 128), 0), iota((128, 128), 1)
    gram = jnp.zeros((128, 128), F32)
    for planes in (slice(0, 8), slice(8, 16)):
        mine_high, mine_low = halves(above[planes].reshape(128, COLS))
        next_high, next_low = halves(top[planes].reshape(128, COLS))
        product = contract(mine_high, jnp.concatenate([next_high, next_low], axis=0), ((1,), (1,)))
        gram = gram + product[:, :128] + product[:, 128:]
        gram = gram + contract(mine_low, next_high, ((1,), (1,)))
    along_rows = diagonal_sums(gram, (row // 16 == col // 16) & (col < row), OFFSETS + lanes(1))
    out[...] = jnp.broadcast_to((sums[...] + only(1, along_rows))[None], out.shape)


def gradient_kernel(
    voxels, field, row_far, row_near, col_early, col_late, totals, targets, weights, gradient, correlation, result, value_ref, sems
):
    value = jnp.sum(totals[...], axis=0, keepdims=True) / jnp.float32(voxels)
    value = jnp.concatenate([value[:, OFFSETS * a : OFFSETS * (a + 1)] for a in range(3)], axis=0)
    value_ref[...] = value
    copies = [pltpu.make_async_copy(value_ref, correlation, sems.at[GROUPS])]
    copies[0].start()
    coefficient = weights[...] * (value - targets[...])
    lane, offset = iota((OFFSETS, 128), 1), iota((OFFSETS, 128), 0)
    same = iota((OFFSETS, OFFSETS), 0) == iota((OFFSETS, OFFSETS), 1)

    def column(axis):
        return jnp.sum(
            jnp.where(same, coefficient[axis : axis + 1], 0.0), axis=1, keepdims=True
        )

    def line(values, lanes):
        return jnp.sum(jnp.where(lane == lanes, values, 0.0), axis=0, keepdims=True)

    def toeplitz(values, size, base):
        return pltpu.roll(
            jnp.broadcast_to(values, (size, 128)), base, 1, stride=1, stride_axis=0
        )

    def both(high, low):
        return jnp.concatenate(
            [
                jnp.concatenate([high, high], axis=1),
                jnp.concatenate([low, jnp.zeros_like(low)], axis=1),
            ],
            axis=0,
        )

    back = (128 - offset) % 128
    nn = ((1,), (0,))
    along_planes, along_rows, along_cols = column(0), column(1), column(2)
    row, col = iota((128, 128), 0), iota((128, 128), 1)
    around = toeplitz(line(along_cols, offset) + line(along_cols, back), 128, 0)
    inside = jnp.abs(col - row) < OFFSETS
    col_high, col_low = halves(
        jnp.concatenate([jnp.where(inside, around, 0.0), jnp.where(inside, 0.0, around)], axis=0)
    )
    row_left = both(
        *halves(
            toeplitz(line(along_rows, offset) + line(along_rows, back), ROWS, OFFSETS)[
                :, : ROWS + 32
            ]
        )
    )
    ahead = toeplitz(line(along_planes, 8 * offset), 128, 0)
    behind = toeplitz(line(along_planes, (128 - 8 * offset) % 128), 128, 0)
    plane_left = both(
        *halves(jnp.where(col == row, 2.0 * ahead, jnp.where(col > row, ahead, behind)))
    )
    below, above = swapped(odd("c"), row_near[...], row_far[...])
    left, right = swapped(odd("c"), col_early[...], col_late[...])

    for pair in range(ROWS // 16):
        parts = []
        for side in range(2):
            rows = slice(16 * pair + 8 * side, 16 * pair + 8 * side + 8)
            parts.append(jnp.concatenate(halves(field[:, rows, :].reshape(128, COLS)), axis=0))
        product = contract(plane_left, jnp.concatenate(parts, axis=1), nn)
        product = product[:128] + product[128:]
        for side in range(2):
            rows = slice(16 * pair + 8 * side, 16 * pair + 8 * side + 8)
            result[:, rows, :] = product[:, COLS * side : COLS * (side + 1)].reshape(PLANES, 8, COLS)

    block = iota((128, COLS), 1) // OFFSETS
    col_right = jnp.concatenate([col_high, col_low], axis=1)
    for group in range(GROUPS):
        values = field[2 * group : 2 * group + 2].reshape(128, COLS)
        halo = jnp.where(block == group, right, left)
        if group:
            halo = pltpu.roll(halo, 128 - OFFSETS * group, 1)
        high, low = halves(jnp.concatenate([values, halo], axis=1))
        product = contract(high, col_right, nn)
        total = product[:, :128] + product[:, 128:] + contract(low, col_high, nn)
        talls = []
        for plane in (2 * group, 2 * group + 1):
            tall = jnp.concatenate([above[plane], field[plane], below[plane]], axis=0)
            talls.append(jnp.concatenate(halves(tall), axis=0))
        product = contract(row_left, jnp.concatenate(talls, axis=1), nn)
        product = product[:ROWS] + product[ROWS:]
        total = total + jnp.concatenate([product[:, :COLS], product[:, COLS:]], axis=0)
        planes = slice(2 * group, 2 * group + 2)
        result[planes] = result[planes] + total.reshape(2, ROWS, COLS)
        copy = pltpu.make_async_copy(result.at[planes], gradient.at[planes], sems.at[group])
        copy.start()
        copies.append(copy)
    for copy in copies:
        copy.wait()


def middle_kernel(parts, out):
    total = jnp.sum(parts[...], axis=0)[:1]
    out[...] = jnp.broadcast_to(total, out.shape)


def pass_on(block, early):
    rows, cols = lax.axis_size(GY), lax.axis_size(GX)
    pairs = []
    for row in range(rows):
        step = 1 if (row % 2 == 0) == early else cols - 1
        pairs += [(row * cols + i, row * cols + (i + step) % cols) for i in range(cols)]
    return lax.ppermute(block, GY + GX, pairs)


def swap(block, axes, shift):
    count = lax.axis_size(axes)
    pairs = [(i, (i + 1) % count) for i in range(shift, count, 2)]
    return lax.ppermute(block, axes, [pair for i, j in pairs for pair in ((i, j), (j, i))])


def exchange(parts, axes):
    if parts.ndim == 2:
        return lax.all_to_all(parts[:, None], axes, 0, 0)[:, 0]
    return lax.all_to_all(parts, axes, 0, 0)


def resident(*shape):
    return pltpu.VMEM(shape, F32)


def near(values):
    return pltpu.with_memory_space_constraint(values, pltpu.VMEM)


def on_device(field, targets, weights):
    voxels = PLANES * ROWS * COLS * lax.axis_size(GY + GX)
    plane_count, line_count = lax.axis_size(PLANE), lax.axis_size(LINE)
    edge = resident(PLANES, OFFSETS, COLS)
    side = resident(128, COLS)
    vmem = pl.BlockSpec(memory_space=pltpu.VMEM)
    field = near(field)
    early, late = pl.pallas_call(
        columns_kernel,
        out_shape=(side, side),
        in_specs=[vmem],
        out_specs=(vmem,) * 2,
        name="columns",
    )(field)
    col_early = near(pass_on(early, True))
    mine_near, mine_far = pl.pallas_call(
        rows_kernel, out_shape=(edge, edge), in_specs=[vmem] * 2, out_specs=(vmem,) * 2, name="rows"
    )(field, near(early))
    row_far = near(swap(mine_far, GY, 1))
    row_near = near(swap(mine_near, GY, 0))
    inner = pl.pallas_call(
        inner_kernel,
        out_shape=resident(1, 128),
        in_specs=[vmem],
        out_specs=vmem,
        name="inner",
        cost_estimate=pl.CostEstimate(flops=INNER, bytes_accessed=1 << 19, transcendentals=0),
    )(field)
    sums = pl.pallas_call(
        border_cols_kernel,
        out_shape=resident(1, 128),
        in_specs=[vmem] * 3,
        out_specs=vmem,
        name="border_cols",
        cost_estimate=pl.CostEstimate(flops=BORDER, bytes_accessed=1 << 17, transcendentals=0),
    )(col_early, near(late), near(inner))
    late_again = pl.pallas_call(
        again_kernel, out_shape=side, in_specs=[vmem] * 2, out_specs=vmem, name="again"
    )(near(late), near(sums))
    col_late = near(pass_on(late_again, False))
    sums = pl.pallas_call(
        border_rows_kernel,
        out_shape=resident(plane_count, PAY, 128),
        in_specs=[vmem] * 5,
        out_specs=vmem,
        name="border_rows",
    )(near(mine_far), near(mine_near), row_far, row_near, near(sums))
    sums = pl.pallas_call(
        middle_kernel,
        out_shape=resident(line_count, 128),
        in_specs=[vmem],
        out_specs=vmem,
        name="middle",
        cost_estimate=pl.CostEstimate(flops=MIDDLE, bytes_accessed=1 << 14, transcendentals=0),
    )(near(exchange(sums, PLANE)))
    totals = near(exchange(sums, LINE))
    return pl.pallas_call(
        lambda *refs: gradient_kernel(voxels, *refs),
        out_shape=(jax.ShapeDtypeStruct((PLANES, ROWS, COLS), F32), jax.ShapeDtypeStruct((3, OFFSETS), F32)),
        in_specs=[vmem] * 8,
        out_specs=(HBM_SPEC, HBM_SPEC),
        scratch_shapes=[
            pltpu.VMEM((PLANES, ROWS, COLS), F32),
            pltpu.VMEM((3, OFFSETS), F32),
            pltpu.SemaphoreType.DMA((GROUPS + 1,)),
        ],
        name="gradient",
    )(field, row_far, row_near, col_early, col_late, totals, near(targets), near(weights))


def solution(mesh):
    devices = np.asarray(mesh.devices).reshape(4, 4, 2, 4, 4)
    fine = Mesh(devices, GY + GX)
    return jax.shard_map(
        on_device,
        mesh=fine,
        in_specs=(P(None, GY, GX), P(), P()),
        out_specs=(P(None, GY, GX), P()),
        check_vma=False,
    )
```

```python
import jax
import jax.numpy as jnp
import numpy as np
from jax import lax
from jax.experimental import pallas as pl
from jax.experimental.pallas import tpu as pltpu
from jax.sharding import Mesh, PartitionSpec as P

OFFSETS = 16
GY = ("zl", "y", "c")
GX = ("x", "zh")
PLANE = ("c", "y", "x")
LINE = ("zl", "zh")
PLANES, ROWS, COLS = 16, 64, 128
GROUPS = 8
F32, BF16 = jnp.float32, jnp.bfloat16
MIDDLE = 3_000_000_000
INNER, BORDER = 600_000_000, 2_000_000_000
HBM_SPEC = pl.BlockSpec(memory_space=pl.ANY)


def iota(shape, dim):
    return lax.broadcasted_iota(jnp.int32, shape, dim)


def halves(values):
    high = values.astype(BF16)
    return high, (values - high.astype(F32)).astype(BF16)


def contract(left, right, dims):
    return lax.dot_general(left, right, (dims, ((), ())), preferred_element_type=F32)


def quadrants(gram):
    half = gram.shape[0] // 2
    tall = gram[:half] + gram[half:]
    return tall[:, :half] + tall[:, half:] if half == 128 else tall + pltpu.roll(tall, half, 1)


def diagonal_sums(gram, keep, base):
    gram = jnp.where(keep, gram, 0.0)
    total = jnp.zeros((8, 128), F32)
    for block in range(gram.shape[0] // 8):
        by = (base - 8 * block) % 128
        values = gram[8 * block : 8 * block + 8]
        total = total + (pltpu.roll(values, by, 1) if by else values)
    row = iota((8, 128), 0)
    moved = jnp.where(row == 0, total, 0.0)
    for step in range(1, 8):
        moved = jnp.where(row == step, pltpu.roll(total, 128 - step, 1), moved)
    return jnp.sum(moved, axis=0, keepdims=True)


def lanes(axis):
    return OFFSETS * axis


def only(axis, sums):
    return jnp.where(iota((1, 128), 1) // OFFSETS == axis, sums, 0.0)


def odd(axis):
    return lax.axis_index(axis) % 2 == 1


def swapped(flag, first, second):
    return jnp.where(flag, second, first), jnp.where(flag, first, second)


def columns_kernel(field, early, late):
    block = iota((128, COLS), 1) // OFFSETS
    first = jnp.zeros((128, COLS), F32)
    last = jnp.zeros((128, COLS), F32)
    for group in range(GROUPS):
        values = field[2 * group : 2 * group + 2].reshape(128, COLS)
        moved = pltpu.roll(values, OFFSETS * group, 1) if group else values
        first = jnp.where(block == group, moved, first)
        last = jnp.where(block == (group + 7) % 8, moved, last)
    early[...], late[...] = swapped(odd("c"), last, first)


def rows_kernel(field, after, near_pair, far_pair):
    near_pair[...], far_pair[...] = swapped(
        odd("c"), field[:, ROWS - OFFSETS :, :], field[:, :OFFSETS, :]
    )


def again_kernel(late, after, out):
    out[...] = late[...]


def inner_kernel(field, out):
    gram = jnp.zeros((256, 256), F32)
    for part in range(ROWS // 8):
        values = field[:, 8 * part : 8 * part + 8, :].reshape(128, COLS)
        both = jnp.concatenate(halves(values), axis=0)
        gram = gram + contract(both, both, ((1,), (1,)))
    row, col = iota((128, 128), 0), iota((128, 128), 1)
    spread = diagonal_sums(quadrants(gram), (row % 8 == col % 8) & (col >= row), 0)
    gram = jnp.zeros((128, 128), F32)
    for plane in range(PLANES):
        both = jnp.concatenate(halves(field[plane]), axis=0)
        gram = gram + contract(both, both, ((1,), (1,)))
    apart = (col - row)[:ROWS]
    along_rows = diagonal_sums(
        quadrants(gram), (apart >= 0) & (apart < OFFSETS) & (col[:ROWS] < ROWS), lanes(1)
    )
    gram = jnp.zeros((256, 256), F32)
    for group in range(GROUPS):
        both = jnp.concatenate(halves(field[2 * group : 2 * group + 2].reshape(128, COLS)), axis=1)
        gram = gram + contract(both, both, ((0,), (0,)))
    apart = col - row
    along_cols = diagonal_sums(quadrants(gram), (apart >= 0) & (apart < OFFSETS), lanes(2))
    lane, offset = iota((OFFSETS, 128), 1), iota((OFFSETS, 128), 0)
    column = jnp.sum(jnp.where(lane == 8 * offset, spread, 0.0), axis=1, keepdims=True)
    along_planes = jnp.sum(jnp.where(lane == offset, column, 0.0), axis=0, keepdims=True)
    out[...] = only(0, along_planes) + only(1, along_rows) + only(2, along_cols)


def border_cols_kernel(received, late, inner, out):
    left, right = swapped(odd("c"), received[...], late[...])
    row, col = iota((128, 128), 0), iota((128, 128), 1)
    mine = jnp.concatenate(halves(left), axis=1)
    other = jnp.concatenate(halves(right), axis=1)
    gram = quadrants(contract(mine, other, ((0,), (0,))))
    apart = (col - row + 128) % 128
    keep = ((row // 16 + 1) % 8 == col // 16) & (apart < OFFSETS) & (apart > 0)
    out[...] = inner[...] + only(2, diagonal_sums(gram, keep, lanes(2)))


def border_rows_kernel(mine_far, mine_near, row_far, row_near, sums, out):
    _, above = swapped(odd("c"), row_near[...], row_far[...])
    _, top = swapped(odd("c"), mine_near[...], mine_far[...])
    row, col = iota((128, 128), 0), iota((128, 128), 1)
    gram = jnp.zeros((128, 128), F32)
    for planes in (slice(0, 8), slice(8, 16)):
        mine_high, mine_low = halves(above[planes].reshape(128, COLS))
        next_high, next_low = halves(top[planes].reshape(128, COLS))
        product = contract(mine_high, jnp.concatenate([next_high, next_low], axis=0), ((1,), (1,)))
        gram = gram + product[:, :128] + product[:, 128:]
        gram = gram + contract(mine_low, next_high, ((1,), (1,)))
    along_rows = diagonal_sums(gram, (row // 16 == col // 16) & (col < row), OFFSETS + lanes(1))
    out[...] = jnp.broadcast_to(sums[...] + only(1, along_rows), out.shape)


def gradient_kernel(
    voxels, field, row_far, row_near, col_early, col_late, totals, targets, weights, gradient, correlation, result, value_ref, sems
):
    value = jnp.sum(totals[...], axis=0, keepdims=True) / jnp.float32(voxels)
    value = jnp.concatenate([value[:, OFFSETS * a : OFFSETS * (a + 1)] for a in range(3)], axis=0)
    value_ref[...] = value
    copies = [pltpu.make_async_copy(value_ref, correlation, sems.at[GROUPS])]
    copies[0].start()
    coefficient = weights[...] * (value - targets[...])
    lane, offset = iota((OFFSETS, 128), 1), iota((OFFSETS, 128), 0)
    same = iota((OFFSETS, OFFSETS), 0) == iota((OFFSETS, OFFSETS), 1)

    def column(axis):
        return jnp.sum(
            jnp.where(same, coefficient[axis : axis + 1], 0.0), axis=1, keepdims=True
        )

    def line(values, lanes):
        return jnp.sum(jnp.where(lane == lanes, values, 0.0), axis=0, keepdims=True)

    def toeplitz(values, size, base):
        return pltpu.roll(
            jnp.broadcast_to(values, (size, 128)), base, 1, stride=1, stride_axis=0
        )

    def both(high, low):
        return jnp.concatenate(
            [
                jnp.concatenate([high, high], axis=1),
                jnp.concatenate([low, jnp.zeros_like(low)], axis=1),
            ],
            axis=0,
        )

    back = (128 - offset) % 128
    nn = ((1,), (0,))
    along_planes, along_rows, along_cols = column(0), column(1), column(2)
    row, col = iota((128, 128), 0), iota((128, 128), 1)
    around = toeplitz(line(along_cols, offset) + line(along_cols, back), 128, 0)
    inside = jnp.abs(col - row) < OFFSETS
    col_high, col_low = halves(
        jnp.concatenate([jnp.where(inside, around, 0.0), jnp.where(inside, 0.0, around)], axis=0)
    )
    row_left = both(
        *halves(
            toeplitz(line(along_rows, offset) + line(along_rows, back), ROWS, OFFSETS)[
                :, : ROWS + 32
            ]
        )
    )
    ahead = toeplitz(line(along_planes, 8 * offset), 128, 0)
    behind = toeplitz(line(along_planes, (128 - 8 * offset) % 128), 128, 0)
    plane_left = both(
        *halves(jnp.where(col == row, 2.0 * ahead, jnp.where(col > row, ahead, behind)))
    )
    below, above = swapped(odd("c"), row_near[...], row_far[...])
    left, right = swapped(odd("c"), col_early[...], col_late[...])

    for pair in range(ROWS // 16):
        parts = []
        for side in range(2):
            rows = slice(16 * pair + 8 * side, 16 * pair + 8 * side + 8)
            parts.append(jnp.concatenate(halves(field[:, rows, :].reshape(128, COLS)), axis=0))
        product = contract(plane_left, jnp.concatenate(parts, axis=1), nn)
        product = product[:128] + product[128:]
        for side in range(2):
            rows = slice(16 * pair + 8 * side, 16 * pair + 8 * side + 8)
            result[:, rows, :] = product[:, COLS * side : COLS * (side + 1)].reshape(PLANES, 8, COLS)

    block = iota((128, COLS), 1) // OFFSETS
    col_right = jnp.concatenate([col_high, col_low], axis=1)
    for group in range(GROUPS):
        values = field[2 * group : 2 * group + 2].reshape(128, COLS)
        halo = jnp.where(block == group, right, left)
        if group:
            halo = pltpu.roll(halo, 128 - OFFSETS * group, 1)
        high, low = halves(jnp.concatenate([values, halo], axis=1))
        product = contract(high, col_right, nn)
        total = product[:, :128] + product[:, 128:] + contract(low, col_high, nn)
        talls = []
        for plane in (2 * group, 2 * group + 1):
            tall = jnp.concatenate([above[plane], field[plane], below[plane]], axis=0)
            talls.append(jnp.concatenate(halves(tall), axis=0))
        product = contract(row_left, jnp.concatenate(talls, axis=1), nn)
        product = product[:ROWS] + product[ROWS:]
        total = total + jnp.concatenate([product[:, :COLS], product[:, COLS:]], axis=0)
        planes = slice(2 * group, 2 * group + 2)
        result[planes] = result[planes] + total.reshape(2, ROWS, COLS)
        copy = pltpu.make_async_copy(result.at[planes], gradient.at[planes], sems.at[group])
        copy.start()
        copies.append(copy)
    for copy in copies:
        copy.wait()


def middle_kernel(parts, out):
    total = jnp.sum(parts[...], axis=0, keepdims=True)
    out[...] = jnp.broadcast_to(total, out.shape)


def pass_on(block, early):
    rows, cols = lax.axis_size(GY), lax.axis_size(GX)
    pairs = []
    for row in range(rows):
        step = 1 if (row % 2 == 0) == early else cols - 1
        pairs += [(row * cols + i, row * cols + (i + step) % cols) for i in range(cols)]
    return lax.ppermute(block, GY + GX, pairs)


def swap(block, axes, shift):
    count = lax.axis_size(axes)
    pairs = [(i, (i + 1) % count) for i in range(shift, count, 2)]
    return lax.ppermute(block, axes, [pair for i, j in pairs for pair in ((i, j), (j, i))])


def exchange(parts, axes):
    if parts.ndim == 2:
        return lax.all_to_all(parts[:, None], axes, 0, 0)[:, 0]
    return lax.all_to_all(parts, axes, 0, 0)


def resident(*shape):
    return pltpu.VMEM(shape, F32)


def near(values):
    return pltpu.with_memory_space_constraint(values, pltpu.VMEM)


def on_device(field, targets, weights):
    voxels = PLANES * ROWS * COLS * lax.axis_size(GY + GX)
    plane_count, line_count = lax.axis_size(PLANE), lax.axis_size(LINE)
    edge = resident(PLANES, OFFSETS, COLS)
    side = resident(128, COLS)
    vmem = pl.BlockSpec(memory_space=pltpu.VMEM)
    field = near(field)
    early, late = pl.pallas_call(
        columns_kernel,
        out_shape=(side, side),
        in_specs=[vmem],
        out_specs=(vmem,) * 2,
        name="columns",
    )(field)
    col_early = near(pass_on(early, True))
    mine_near, mine_far = pl.pallas_call(
        rows_kernel, out_shape=(edge, edge), in_specs=[vmem] * 2, out_specs=(vmem,) * 2, name="rows"
    )(field, near(early))
    row_far = near(swap(mine_far, GY, 1))
    row_near = near(swap(mine_near, GY, 0))
    inner = pl.pallas_call(
        inner_kernel,
        out_shape=resident(1, 128),
        in_specs=[vmem],
        out_specs=vmem,
        name="inner",
        cost_estimate=pl.CostEstimate(flops=INNER, bytes_accessed=1 << 19, transcendentals=0),
    )(field)
    sums = pl.pallas_call(
        border_cols_kernel,
        out_shape=resident(1, 128),
        in_specs=[vmem] * 3,
        out_specs=vmem,
        name="border_cols",
        cost_estimate=pl.CostEstimate(flops=BORDER, bytes_accessed=1 << 17, transcendentals=0),
    )(col_early, near(late), near(inner))
    late_again = pl.pallas_call(
        again_kernel, out_shape=side, in_specs=[vmem] * 2, out_specs=vmem, name="again"
    )(near(late), near(sums))
    col_late = near(pass_on(late_again, False))
    sums = pl.pallas_call(
        border_rows_kernel,
        out_shape=resident(plane_count, 128),
        in_specs=[vmem] * 5,
        out_specs=vmem,
        name="border_rows",
    )(near(mine_far), near(mine_near), row_far, row_near, near(sums))
    sums = pl.pallas_call(
        middle_kernel,
        out_shape=resident(line_count, 128),
        in_specs=[vmem],
        out_specs=vmem,
        name="middle",
        cost_estimate=pl.CostEstimate(flops=MIDDLE, bytes_accessed=1 << 14, transcendentals=0),
    )(near(exchange(sums, PLANE)))
    totals = near(exchange(sums, LINE))
    return pl.pallas_call(
        lambda *refs: gradient_kernel(voxels, *refs),
        out_shape=(jax.ShapeDtypeStruct((PLANES, ROWS, COLS), F32), jax.ShapeDtypeStruct((3, OFFSETS), F32)),
        in_specs=[vmem] * 8,
        out_specs=(HBM_SPEC, HBM_SPEC),
        scratch_shapes=[
            pltpu.VMEM((PLANES, ROWS, COLS), F32),
            pltpu.VMEM((3, OFFSETS), F32),
            pltpu.SemaphoreType.DMA((GROUPS + 1,)),
        ],
        name="gradient",
    )(field, row_far, row_near, col_early, col_late, totals, near(targets), near(weights))


def solution(mesh):
    devices = np.asarray(mesh.devices).reshape(4, 4, 2, 4, 4)
    fine = Mesh(devices, GY + GX)
    return jax.shard_map(
        on_device,
        mesh=fine,
        in_specs=(P(None, GY, GX), P(), P()),
        out_specs=(P(None, GY, GX), P()),
        check_vma=False,
    )
```
